32 devices in a mesh: group: 2 (over y), dm: 4 (over z), tm: 2 (over x), beam: 2 (over core).
Axes of the slice: x: 2, y: 2, z: 4, core: 2. Of those that a mesh axis runs over, the one named last changes fastest.
Arguments:
- raw: bfloat16 [16, 4194304], P(('group', 'dm', 'beam'), 'tm'), parts along dimension 0
- proto: float32 [4, 16384], replicated, may hold values from -4 to 4
- delays: int32 [8, 4, 64], replicated, may hold values from 0 to 3, as said below
- widths: int32 [8], replicated, may hold values from 1 to 8, as said below
- owners: int32 [8, 1], replicated, may hold values from 0 to 3; in each aligned block of 8 rows (0 to 7, 8 to 15, ...) at most 4 rows name the same one
Outputs:
- detect: bfloat16 [16, 8, 2, 4, 8, 256], P('dm', 'group', 'beam', None, None, 'tm'), parts along dimension 1
The draws below stay inside these ranges and needn't reach their ends.
There are 2 independent parts, one for each index of `group`. The reference program is written for one: setup_inputs(seed, part) draws one part's arguments, and reference() takes and returns one part's arrays. A program takes and returns all parts, laid end to end along the dimension named above; an argument that names none is the same for every part. Nothing has to cross between parts.
Inputs may be any that keep to these rules, and one draw needn't show every extreme that they name: `delays`: 3 occurs in every draw. `widths`: 8 occurs in every draw. `owners`: each owner holds at most 4 DM blocks, and some owner holds exactly 4.
All inputs are finite; a program needn't handle non-finite values.
Results may differ from the reference program's by a relative error of at most 0.014.
Values may be sent and summed in bfloat16 or wider, within the bound.
A program may use at most 128 MiB of HBM per device.

```python
import math
import jax
import jax.numpy as jnp
import numpy as np
from jax import lax

NCH = 16384
DFT_A = 128
DFT_B = 128
TAPS = 4
NBLK = 64
CBW = 256
SPECTRA = 256
SAMPLES = 4194304
BEAM_SUB = 2
BEAMS = 8
PFB_BLK = 16
FD = 4
TT = 8
MAXT = 3
WMAX = 8
NBOX = 8
TRIALS = 4
NDMB = 8
CAP = 4
SLOTS = 16
HALO = 31
N_DM = 4


def draw_raw(key, part):
    key_noise = jax.random.fold_in(key, 11)
    key_level = jax.random.fold_in(key, 12)
    steps = jnp.arange(SPECTRA, dtype=jnp.float32) / max(SPECTRA - 1, 1)
    jitter = jax.random.uniform(key_level, (BEAMS, SPECTRA, 1), jnp.float32)
    values = jax.random.normal(key_noise, (BEAMS, SPECTRA, NCH), jnp.float32)
    level = jnp.power(10.0, 0.5 * steps[None, :, None] + 0.5 * jitter)
    return (values * jnp.sqrt(level)).reshape(BEAMS, SAMPLES).astype(jnp.bfloat16)


def draw_delays(key, part):
    block = jnp.arange(NDMB, dtype=jnp.int32)[:, None, None]
    trial = jnp.arange(TRIALS, dtype=jnp.int32)[None, :, None]
    channel = jnp.arange(NBLK, dtype=jnp.int32)[None, None, :]
    level = block * TRIALS + trial
    base = level * (NBLK - 1 - channel) * MAXT // max((NDMB * TRIALS - 1) * (NBLK - 1), 1)
    jitter = jax.random.randint(jax.random.fold_in(key, 21), (NDMB, TRIALS, NBLK), 0, 2)
    return jnp.minimum(base + jitter, MAXT).astype(jnp.int32)


def draw_widths(key, part):
    values = jax.random.randint(jax.random.fold_in(key, 31), (NBOX,), 1, WMAX + 1)
    where_top = jax.random.randint(jax.random.fold_in(key, 32), (), 0, NBOX)
    index = jnp.arange(NBOX, dtype=jnp.int32)
    return jnp.where(index == where_top, WMAX, values).astype(jnp.int32)


def shared_out(own_key, own, number, rows, amount, top, reach, skew):
    sequence = jax.random.permutation(own_key, amount)
    packed, usual = portions_of(amount, rows * top, reach, skew, True), portions_of(amount, rows * top, reach, skew, False)
    places = jnp.arange(amount)

    def named(tallies, rotation):
        used = int((tallies > 0).sum())
        fixed = max(1, used // 4)
        moved = fixed + (places - fixed + rotation * (used - fixed)) % max(1, amount - fixed)
        return jnp.zeros((amount,), jnp.int32).at[sequence[jnp.where(places < fixed, places, moved)]].set(jnp.asarray(tallies, jnp.int32))

    tallies = jnp.where(number % 4 == 0, named(packed, number // 4), named(usual, number - number // 4 - 1))
    mixed = jax.random.permutation(jax.random.fold_in(own, 3), amount)
    donor, taker = mixed[0:amount // 2 * 2:2], mixed[1:amount // 2 * 2:2]
    room = jnp.minimum(tallies[donor] - 1, reach - tallies[taker]) // 2
    room = jnp.where((donor == sequence[0]) | (taker == sequence[0]) | (tallies[taker] == 0), 0, jnp.maximum(room, 0))
    moved = jax.random.randint(jax.random.fold_in(own, 4), (amount // 2,), 0, 1 << 20) % (room + 1)
    tallies = tallies.at[donor].add(-moved).at[taker].add(moved)
    members = jnp.searchsorted(jnp.cumsum(tallies), jnp.arange(rows * top), side="right").astype(jnp.int32)
    table = members.reshape(top, rows).T
    table = table[jax.random.permutation(jax.random.fold_in(own, 1), rows)]
    rotation = jax.random.randint(jax.random.fold_in(own, 2), (rows, 1), 0, top)
    return jnp.take_along_axis(table, (jnp.arange(top)[None, :] + rotation) % top, axis=1)


def portions_of(number_of, total, bound, skew, full):
    weights = [(1 << 20) // math.isqrt(rank ** skew) + 1 for rank in range(1, number_of + 1)]
    largest = bound if full else min(bound, max(-(-total // number_of), total * weights[0] // sum(weights)))
    least = 1 if total - largest >= number_of - 1 else 0
    counts, rest = [largest] + [least] * (number_of - 1), total - largest - least * (number_of - 1)
    while rest > 0:
        candidates = [i for i in range(1, number_of) if counts[i] < largest] or [i for i in range(1, number_of) if counts[i] < bound]
        pool, budget = sum([weights[i] for i in candidates]), rest
        for i in candidates:
            more = min(bound - counts[i], max(1, budget * weights[i] // pool), rest)
            counts[i] = counts[i] + more
            rest = rest - more
    return np.array(counts)


def centred(rng, shape, scale, bound, held_as=jnp.bfloat16):
    values = jax.random.normal(rng, shape, jnp.float32) * scale
    return jnp.minimum(jnp.maximum(values, -bound), bound).astype(held_as)


def setup_inputs(seed: int = 0, part: int = 0) -> dict:
    seeds = jax.random.split(jax.random.key(seed), 6)
    part_keys = jax.random.split(jax.random.fold_in(seeds[5], part), 6)
    raw = draw_raw(jax.random.fold_in(jax.random.fold_in(seeds[5], part), 71), part)
    proto = centred(seeds[1], (TAPS, NCH), 1.0, 4.0, jnp.float32)
    delays = draw_delays(jax.random.fold_in(seeds[5], 71), part)
    widths = draw_widths(jax.random.fold_in(seeds[5], 71), part)
    owners_keys = jax.random.split(jax.random.fold_in(seeds[4], 1), NDMB // NDMB)
    owners_turns = jax.random.permutation(jax.random.fold_in(seeds[4], 3), NDMB // NDMB)
    owners = jax.vmap(lambda own, number: shared_out(jax.random.fold_in(seeds[4], 2), own, number, NDMB, N_DM, 1, CAP, 2))(owners_keys, owners_turns).reshape((NDMB, 1))
    return dict(raw=raw, proto=proto, delays=delays, widths=widths, owners=owners)


def dft_tables(size):
    index = jnp.arange(size, dtype=jnp.int32)
    product = index[:, None] * index[None, :] % size
    angle = product.astype(jnp.float32) * (2.0 * math.pi / size)
    return (jnp.cos(angle).astype(jnp.bfloat16), jnp.sin(angle).astype(jnp.bfloat16))

def twiddle_tables(rows, cols, total):
    first = jnp.arange(rows, dtype=jnp.int32)
    second = jnp.arange(cols, dtype=jnp.int32)
    product = first[:, None] * second[None, :] % total
    angle = product.astype(jnp.float32) * (2.0 * math.pi / total)
    return (jnp.cos(angle), jnp.sin(angle))

def spectra_power(window_frames, proto):
    count = window_frames.shape[0] - TAPS + 1
    hp = lax.Precision.HIGHEST
    acc = window_frames[0:count].astype(jnp.float32) * proto[0]
    for tap in range(1, TAPS):
        acc = acc + window_frames[tap:tap + count].astype(jnp.float32) * proto[tap]
    frames_bf = acc.astype(jnp.bfloat16).astype(jnp.float32).reshape(count, DFT_A, DFT_B)
    cos_a, sin_a = dft_tables(DFT_A)
    cos_b, sin_b = dft_tables(DFT_B)
    tw_cos, tw_sin = twiddle_tables(DFT_B, DFT_A, NCH)
    a_re = jnp.einsum('kab,fa->kbf', frames_bf, cos_a.astype(jnp.float32), precision=hp)
    a_im = -jnp.einsum('kab,fa->kbf', frames_bf, sin_a.astype(jnp.float32), precision=hp)
    t_re = (a_re * tw_cos + a_im * tw_sin).astype(jnp.bfloat16).astype(jnp.float32)
    t_im = (a_im * tw_cos - a_re * tw_sin).astype(jnp.bfloat16).astype(jnp.float32)
    cb = cos_b.astype(jnp.float32)
    sb = sin_b.astype(jnp.float32)
    c_re = jnp.einsum('kbf,gb->kgf', t_re, cb, precision=hp) + jnp.einsum('kbf,gb->kgf', t_im, sb, precision=hp)
    c_im = jnp.einsum('kbf,gb->kgf', t_im, cb, precision=hp) - jnp.einsum('kbf,gb->kgf', t_re, sb, precision=hp)
    power = (c_re * c_re + c_im * c_im) * (1.0 / (TAPS * NCH))
    return power.reshape(count, NCH)

def fine_masks(groups, width):
    block = jnp.arange(groups, dtype=jnp.int32)[:, None]
    inner = jnp.arange(width, dtype=jnp.int32)[None, :]
    fine = block * FD * (width - 1 - inner) // (groups * (width - 1))
    return jnp.stack([(fine == step).astype(jnp.float32) for step in range(FD)])

def beam_subbands(samples, proto, masks):
    frames = samples.reshape(SPECTRA, NCH)
    padded = jnp.concatenate([jnp.zeros((TAPS - 1, NCH), jnp.bfloat16), frames], 0)

    def block_power(index):
        start = (index * PFB_BLK).astype(jnp.int32)
        window = lax.dynamic_slice_in_dim(padded, start, PFB_BLK + TAPS - 1, 0)
        return spectra_power(window, proto)
    power = lax.map(block_power, jnp.arange(SPECTRA // PFB_BLK, dtype=jnp.int32)).reshape(SPECTRA, NCH)
    band = lax.optimization_barrier(jnp.sum(power, 0)) / SPECTRA
    ratio = power / (band + 1e-06)
    flat = (ratio - lax.optimization_barrier(jnp.mean(ratio, 1, keepdims=True))).astype(jnp.bfloat16)
    flat = jnp.concatenate([jnp.zeros((FD - 1, NCH), jnp.bfloat16), flat], 0)
    view = flat.reshape(SPECTRA + FD - 1, NBLK, CBW).astype(jnp.float32)
    total = jnp.zeros((NDMB, NBLK, SPECTRA), jnp.float32)
    for step in range(FD):
        part = view[FD - 1 - step:FD - 1 - step + SPECTRA]
        total = total + jnp.einsum('kci,gi->gck', part, masks[step], precision=lax.Precision.HIGHEST)
    return (total * (1.0 / math.sqrt(CBW))).astype(jnp.bfloat16)

def dedisperse(extended, delays, count):
    length = count + WMAX - 1
    total = 0.0
    for value in range(MAXT + 1):
        start = (MAXT - value) * TT
        window = extended[..., start:start + length].astype(jnp.float32)
        mask = (delays == value).astype(jnp.float32)
        total = total + jnp.einsum('rgck,gjc->rgjk', window, mask, precision=lax.Precision.HIGHEST)
    return total * (1.0 / math.sqrt(NBLK))

def boxcar(series, widths, count):
    lags = jnp.arange(WMAX, dtype=jnp.int32)
    weights = (lags[None, :] < widths[:, None]).astype(jnp.float32) / jnp.sqrt(widths.astype(jnp.float32))[:, None]
    stacked = jnp.stack([series[..., WMAX - 1 - lag:WMAX - 1 - lag + count] for lag in range(WMAX)], -2)
    return jnp.einsum('rgjik,wi->rgjwk', stacked, weights, precision=lax.Precision.HIGHEST)

def slot_table(owners, owner_count, capacity):
    owner = owners[:, 0]
    groups = owner.shape[0]
    index = jnp.arange(groups, dtype=jnp.int32)
    same = owner[:, None] == owner[None, :]
    earlier = index[None, :] < index[:, None]
    rank = lax.optimization_barrier(jnp.sum((same & earlier).astype(jnp.int32), 1))
    hit_owner = owner[None, None, :] == jnp.arange(owner_count, dtype=jnp.int32)[:, None, None]
    hit_slot = rank[None, None, :] == jnp.arange(capacity, dtype=jnp.int32)[None, :, None]
    return (hit_owner & hit_slot).astype(jnp.int32)

def reference(raw, proto, delays, widths, owners):
    masks = fine_masks(NDMB, CBW)

    def one_beam(samples):
        return beam_subbands(samples, proto, masks)
    subs = lax.map(one_beam, raw)
    extended = jnp.concatenate([jnp.zeros((BEAMS, NDMB, NBLK, HALO), jnp.bfloat16), subs], -1)
    series = dedisperse(extended, delays, SPECTRA)
    box = boxcar(series, widths, SPECTRA).astype(jnp.bfloat16)
    table = slot_table(owners, N_DM, CAP).astype(jnp.float32)
    placed = jnp.einsum('osg,rgjwk->osrjwk', table, box.astype(jnp.float32), precision=lax.Precision.HIGHEST)
    return placed.reshape(SLOTS, N_DM, BEAM_SUB, TRIALS, NBOX, SPECTRA).astype(jnp.bfloat16)
```

```python
import functools
import math

import jax
import jax.numpy as jnp
import numpy as np
from jax import lax
from jax.experimental import pallas as pl
from jax.experimental.pallas import tpu as pltpu
from jax.sharding import PartitionSpec as P

SIDE = 128
NBLK = 64
FD = 4
TT = 8
MAXT = 3
WMAX = 8
SPB = 8
F32 = jnp.float32
BF16 = jnp.bfloat16


def shifted(value, axis, steps):
    count = lax.axis_size(axis)
    return lax.ppermute(value, axis, [(s, s + steps) for s in range(count - steps)])


def tables(channels):
    i = np.arange(SIDE)
    ang = (i[:, None] * i[None, :] % SIDE) * (2.0 * math.pi / SIDE)
    c, s = np.cos(ang), np.sin(ang)
    w1 = np.concatenate([c, s], 0)
    w2 = np.block([[c, -s], [-s, -c]])
    tw = (i[:, None] * i[None, :] % channels) * (2.0 * math.pi / channels)
    twiddle = np.stack([np.cos(tw), np.sin(tw)]).astype(np.float32)
    return jnp.asarray(w1, BF16), jnp.asarray(w2, BF16), jnp.asarray(twiddle)


def fine_rows(groups, width):
    g = np.arange(groups)[:, None]
    i = np.arange(width)[None, :]
    fine = g * FD * (width - 1 - i) // (groups * (width - 1))
    hot = np.stack([fine == step for step in range(FD)])
    hot = hot.reshape(FD, groups, width // SIDE, SIDE).transpose(2, 0, 1, 3)
    return jnp.asarray(hot.reshape(-1, SIDE), BF16)


def front_kernel(scale, x_ref, halo_ref, proto_ref, w1_ref, w2_ref, tw_ref, p_ref, band_ref, carry):
    step = pl.program_id(0)

    @pl.when(step == 0)
    def _():
        carry[...] = halo_ref[...]
        band_ref[...] = jnp.zeros_like(band_ref)

    def frame(index):
        if index < 0:
            return carry[(index + 3) * SIDE : (index + 4) * SIDE]
        return x_ref[index * SIDE : (index + 1) * SIDE]

    total = None
    for s in range(0, SPB, 2):
        ys = []
        for k in (s, s + 1):
            acc = frame(k - 3) * proto_ref[0]
            for tap in range(1, 4):
                acc = acc + frame(k - 3 + tap) * proto_ref[tap]
            ys.append(acc.astype(BF16))
        a = jnp.dot(w1_ref[...], jnp.concatenate(ys, 1), preferred_element_type=F32)
        ts = []
        for m in range(2):
            re = a[:SIDE, m * SIDE : (m + 1) * SIDE]
            im = a[SIDE:, m * SIDE : (m + 1) * SIDE]
            t_re = re * tw_ref[0] - im * tw_ref[1]
            t_ni = im * tw_ref[0] + re * tw_ref[1]
            ts.append(jnp.concatenate([t_re.astype(BF16), t_ni.astype(BF16)], 1))
        c = jnp.dot(jnp.concatenate(ts, 0), w2_ref[...], preferred_element_type=F32)
        re, im = c[:, :SIDE], c[:, SIDE:]
        power = (re * re + im * im) * scale
        p_ref[s * SIDE : (s + 2) * SIDE] = power
        both = power[:SIDE] + power[SIDE:]
        total = both if total is None else total + both
    band_ref[...] += total
    carry[...] = x_ref[(SPB - 3) * SIDE :]


def front(x, halo, proto):
    taps, channels = proto.shape
    rows = x.shape[0]
    w1, w2, tw = tables(channels)
    full = lambda shape: pl.BlockSpec(shape, lambda i: (0,) * len(shape))
    return pl.pallas_call(
        functools.partial(front_kernel, 1.0 / (taps * channels)),
        grid=(rows // (SPB * SIDE),),
        in_specs=[
            pl.BlockSpec((SPB * SIDE, SIDE), lambda i: (i, 0)),
            full(halo.shape),
            full((taps, SIDE, SIDE)),
            full(w1.shape),
            full(w2.shape),
            full(tw.shape),
        ],
        out_specs=[pl.BlockSpec((SPB * SIDE, SIDE), lambda i: (i, 0)), full((SIDE, SIDE))],
        out_shape=[
            jax.ShapeDtypeStruct((rows, SIDE), F32),
            jax.ShapeDtypeStruct((SIDE, SIDE), F32),
        ],
        scratch_shapes=[pltpu.VMEM(halo.shape, F32)],
        compiler_params=pltpu.CompilerParams(vmem_limit_bytes=32 << 20),
        name="front",
    )(x, halo, proto.reshape(taps, SIDE, SIDE), w1, w2, tw)


def flat_kernel(spectra, groups, p_ref, band_ref, m_ref, tot_ref, inv):
    step = pl.program_id(0)

    @pl.when(step == 0)
    def _():
        inv[...] = 1.0 / (band_ref[...] * (1.0 / spectra) + 1e-06)
        tot_ref[...] = jnp.zeros_like(tot_ref)

    even = lax.broadcasted_iota(jnp.int32, (FD * groups, SIDE), 1) % 2 == 0
    for s in range(0, SPB, 2):
        flats = []
        for k in (s, s + 1):
            ratio = p_ref[k * SIDE : (k + 1) * SIDE] * inv[...]
            mean = jnp.sum(jnp.sum(ratio, 0, keepdims=True), 1, keepdims=True) * (1.0 / (SIDE * SIDE))
            flats.append((ratio - mean).astype(BF16))
        r = jnp.dot(m_ref[...], jnp.concatenate(flats, 1), preferred_element_type=F32)
        for m in range(2):
            part = r[:, m * SIDE : (m + 1) * SIDE]
            part = jnp.where(even, part[: FD * groups], part[FD * groups :])
            for d in range(FD):
                tot_ref[step * SPB + s + m + d] += part[d * groups : (d + 1) * groups]


def flat_sums(power, band, groups, spectra):
    spec = power.shape[0] // SIDE
    masks = fine_rows(groups, SIDE * SIDE // NBLK)
    full = lambda shape: pl.BlockSpec(shape, lambda i: (0,) * len(shape))
    out = (spec + FD - 1, groups, SIDE)
    return pl.pallas_call(
        functools.partial(flat_kernel, spectra, groups),
        grid=(spec // SPB,),
        in_specs=[
            pl.BlockSpec((SPB * SIDE, SIDE), lambda i: (i, 0)),
            full((SIDE, SIDE)),
            full(masks.shape),
        ],
        out_specs=full(out),
        out_shape=jax.ShapeDtypeStruct(out, F32),
        scratch_shapes=[pltpu.VMEM((SIDE, SIDE), F32)],
        compiler_params=pltpu.CompilerParams(vmem_limit_bytes=32 << 20),
        name="flatten",
    )(power, band, masks)


def trial_kernel(groups, spec, tail_ref, tot_ref, mask_ref, pack_ref, out_ref):
    quad = (MAXT + 1) * groups
    halo = MAXT * TT + WMAX - 1
    rows = spec + halo + 1
    ext = jnp.concatenate(
        [
            jnp.zeros((1, groups, SIDE), F32),
            tail_ref[:halo],
            tot_ref[: FD - 1] + tail_ref[halo:],
            tot_ref[FD - 1 : spec],
        ],
        0,
    ).reshape(rows * groups, SIDE)
    width = SIDE * SIDE // NBLK
    sub = ((ext + pltpu.roll(ext, SIDE - 1, 1)) * (1.0 / math.sqrt(width))).astype(BF16)
    prod = jnp.dot(sub, mask_ref[...], preferred_element_type=F32)
    lanes = prod.shape[1]
    prod = prod.reshape(rows, groups, lanes)
    lane = lax.broadcasted_iota(jnp.int32, (groups, lanes), 1)
    row = lax.broadcasted_iota(jnp.int32, (groups, lanes), 0)
    own = (lane // 4) % groups == row
    each = jnp.sum(jnp.where(own[None], prod, 0.0), 1)
    count = spec + TT
    dd = 0.0
    for value in range(MAXT + 1):
        start = (MAXT - value) * TT
        dd = dd + each[start : start + count, value * quad : (value + 1) * quad]
    dd = dd * (1.0 / math.sqrt(NBLK))
    wide = pack_ref.shape[1]
    if quad < wide:
        dd = jnp.concatenate([dd, jnp.zeros((count, wide - quad), F32)], 1)
    dd = jnp.concatenate([dd, jnp.zeros((2 * SIDE - count, wide), F32)], 0)
    out_ref[...] = jnp.dot(
        pack_ref[...], dd.T, preferred_element_type=F32, precision=lax.Precision.HIGHEST
    )


def trials_packed(tail, tot, mask, pack, groups, spec):
    return pl.pallas_call(
        functools.partial(trial_kernel, groups, spec),
        out_shape=jax.ShapeDtypeStruct((pack.shape[0], 2 * SIDE), F32),
        compiler_params=pltpu.CompilerParams(vmem_limit_bytes=48 << 20),
        name="trials",
    )(tail, tot, mask, pack)


def box_kernel(got_ref, weight_ref, out_ref):
    rows = got_ref.shape[0]
    got = got_ref[...]
    for n in range(rows // 8):
        part = got[n * 8 : (n + 1) * 8]
        acc = 0.0
        for lag in range(WMAX):
            moved = pltpu.roll(part, 2 * SIDE - (TT - lag), 1)[:, :SIDE]
            acc = acc + moved[:, None, :] * weight_ref[lag][None]
        out_ref[n * 8 : (n + 1) * 8] = acc


def boxcars(got, widths):
    lags = jnp.arange(WMAX, dtype=jnp.int32)
    weights = (lags[:, None] < widths[None, :]).astype(F32) / jnp.sqrt(widths.astype(F32))[None, :]
    weights = jnp.broadcast_to(weights[:, :, None], (WMAX, widths.shape[0], SIDE))
    return pl.pallas_call(
        box_kernel,
        out_shape=jax.ShapeDtypeStruct((got.shape[0], widths.shape[0], SIDE), F32),
        compiler_params=pltpu.CompilerParams(vmem_limit_bytes=32 << 20),
        name="boxcars",
    )(got, weights)


def slot_table(owners, owner_count, capacity):
    owner = owners[:, 0]
    index = jnp.arange(owner.shape[0], dtype=jnp.int32)
    same = owner[:, None] == owner[None, :]
    rank = jnp.sum((same & (index[None, :] < index[:, None])).astype(jnp.int32), 1)
    slot = owner * capacity + rank
    return slot[None, :] == jnp.arange(owner_count * capacity, dtype=jnp.int32)[:, None]


def shards(raw, proto, delays, widths, owners):
    taps, channels = proto.shape
    spec = raw.shape[1] // channels
    groups, trials, _ = delays.shape
    owner_count = lax.axis_size("dm")
    capacity = 2 * (groups // owner_count)
    spectra = spec * lax.axis_size("tm")
    halo = MAXT * TT + WMAX - 1

    before = shifted(raw[:, raw.shape[1] - (taps - 1) * channels :], "tm", 1)
    before = lax.optimization_barrier(before.astype(F32)).reshape(-1, SIDE)
    frames = lax.optimization_barrier(raw.astype(F32)).reshape(-1, SIDE)
    power, band = front(frames, before, proto)
    band = lax.psum(band, "tm")
    tot = flat_sums(power, band, groups, spectra)
    tail = shifted(tot[spec - halo :], "tm", 1)

    value = jnp.arange(MAXT + 1, dtype=jnp.int32)[:, None, None, None]
    hit = (delays[None] == value).reshape(-1, NBLK).T
    mask = jnp.stack([hit, jnp.zeros_like(hit)], 1).reshape(SIDE, -1).astype(BF16)
    table = slot_table(owners, owner_count, capacity)
    pack = table[:, None, :, None] & jnp.eye(trials, dtype=bool)[None, :, None, :]
    pack = pack.reshape(owner_count * capacity * trials, groups * trials).astype(F32)
    pack = jnp.pad(pack, ((0, 0), (0, -pack.shape[1] % SIDE)))

    packed = trials_packed(tail, tot, mask, pack, groups, spec)
    packed = packed.reshape(owner_count, capacity * trials, 2 * SIDE)
    got = lax.all_to_all(packed, "dm", split_axis=0, concat_axis=0, tiled=True)
    box = boxcars(got.reshape(-1, 2 * SIDE), widths)
    box = box.reshape(owner_count, capacity, 1, trials, widths.shape[0], spec)
    return jnp.transpose(box, (1, 0, 2, 3, 4, 5)).astype(BF16)


def solution(mesh):
    return jax.shard_map(
        shards,
        mesh=mesh,
        in_specs=(P(("group", "dm", "beam"), "tm"), P(), P(), P(), P()),
        out_specs=P("dm", "group", "beam", None, None, "tm"),
        check_vma=False,
    )
```

```python
import functools
import math

import jax
import jax.numpy as jnp
import numpy as np
from jax import lax
from jax.experimental import pallas as pl
from jax.experimental.pallas import tpu as pltpu
from jax.sharding import PartitionSpec as P

SIDE = 128
NBLK = 64
FD = 4
TT = 8
MAXT = 3
WMAX = 8
SPB = 8
MESH = pl.DeviceIdType.MESH
F32 = jnp.float32
BF16 = jnp.bfloat16


def shifted(value, axis, steps):
    count = lax.axis_size(axis)
    return lax.ppermute(value, axis, [(s, s + steps) for s in range(count - steps)])


def tables(channels):
    i = np.arange(SIDE)
    ang = (i[:, None] * i[None, :] % SIDE) * (2.0 * math.pi / SIDE)
    c, s = np.cos(ang), np.sin(ang)
    w1 = np.concatenate([c, s], 0)
    w2 = np.block([[c, -s], [-s, -c]])
    tw = (i[:, None] * i[None, :] % channels) * (2.0 * math.pi / channels)
    twiddle = np.stack([np.cos(tw), np.sin(tw)]).astype(np.float32)
    return jnp.asarray(w1, BF16), jnp.asarray(w2, BF16), jnp.asarray(twiddle)


def fine_rows(groups, width):
    g = np.arange(groups)[:, None]
    i = np.arange(width)[None, :]
    fine = g * FD * (width - 1 - i) // (groups * (width - 1))
    hot = np.stack([fine == step for step in range(FD)])
    hot = hot.reshape(FD, groups, width // SIDE, SIDE).transpose(2, 0, 1, 3)
    return jnp.asarray(hot.reshape(-1, SIDE), BF16)


def front_kernel(scale, x_ref, halo_ref, proto_ref, w1_ref, w2_ref, tw_ref, p_ref, band_ref, window):
    step = pl.program_id(0)

    def unfold(ref, index):
        line = ref[:, index * SIDE * SIDE : (index + 1) * SIDE * SIDE]
        return line.astype(F32).reshape(SIDE, SIDE)

    @pl.when(step == 0)
    def _():
        for k in range(3):
            window[k * SIDE : (k + 1) * SIDE] = unfold(halo_ref, k)
        band_ref[...] = jnp.zeros_like(band_ref)

    def frame(index):
        return window[(index + 3) * SIDE : (index + 4) * SIDE]

    total = None
    for s in range(0, SPB, 2):
        for k in (s, s + 1):
            window[(k + 3) * SIDE : (k + 4) * SIDE] = unfold(x_ref, k)
        ys = []
        for k in (s, s + 1):
            acc = frame(k - 3) * proto_ref[0]
            for tap in range(1, 4):
                acc = acc + frame(k - 3 + tap) * proto_ref[tap]
            ys.append(acc.astype(BF16))
        a = jnp.dot(w1_ref[...], jnp.concatenate(ys, 1), preferred_element_type=F32)
        ts = []
        for m in range(2):
            re = a[:SIDE, m * SIDE : (m + 1) * SIDE]
            im = a[SIDE:, m * SIDE : (m + 1) * SIDE]
            t_re = re * tw_ref[0] - im * tw_ref[1]
            t_ni = im * tw_ref[0] + re * tw_ref[1]
            ts.append(jnp.concatenate([t_re.astype(BF16), t_ni.astype(BF16)], 1))
        c = jnp.dot(jnp.concatenate(ts, 0), w2_ref[...], preferred_element_type=F32)
        re, im = c[:, :SIDE], c[:, SIDE:]
        power = (re * re + im * im) * scale
        p_ref[s * SIDE : (s + 2) * SIDE] = power
        both = power[:SIDE] + power[SIDE:]
        total = both if total is None else total + both
    band_ref[...] += total
    window[: 3 * SIDE] = window[SPB * SIDE :]


def front(x, halo, proto):
    taps, channels = proto.shape
    rows = x.shape[1] // SIDE
    w1, w2, tw = tables(channels)
    full = lambda shape: pl.BlockSpec(shape, lambda i: (0,) * len(shape))
    return pl.pallas_call(
        functools.partial(front_kernel, 1.0 / (taps * channels)),
        grid=(rows // (SPB * SIDE),),
        in_specs=[
            pl.BlockSpec((1, SPB * SIDE * SIDE), lambda i: (0, i)),
            full(halo.shape),
            full((taps, SIDE, SIDE)),
            full(w1.shape),
            full(w2.shape),
            full(tw.shape),
        ],
        out_specs=[pl.BlockSpec((SPB * SIDE, SIDE), lambda i: (i, 0)), full((SIDE, SIDE))],
        out_shape=[
            jax.ShapeDtypeStruct((rows, SIDE), F32),
            jax.ShapeDtypeStruct((SIDE, SIDE), F32),
        ],
        scratch_shapes=[pltpu.VMEM(((SPB + 3) * SIDE, SIDE), F32)],
        compiler_params=pltpu.CompilerParams(vmem_limit_bytes=40 << 20),
        name="front",
    )(x, halo, proto.reshape(taps, SIDE, SIDE), w1, w2, tw)


def search_kernel(
    sizes, p_ref, band_ref, m_ref, mask_ref, pack_ref, weight_ref, out_ref,
    bands, inv, tot, tail, send, got, band_send, band_recv, tail_send, tail_recv, own_send, own_recv,
):
    spectra, spec, groups, slabs, owner_count, axes = sizes
    halo = MAXT * TT + WMAX - 1
    quad = (MAXT + 1) * groups
    tm, dm = lax.axis_index("tm"), lax.axis_index("dm")

    def peer(axis, shift):
        place = {name: lax.axis_index(name) for name in axes}
        place[axis] = lax.rem(place[axis] + shift, lax.axis_size(axis))
        return tuple(place[name] for name in axes)

    barrier = pltpu.get_barrier_semaphore()
    for off in range(1, slabs):
        pl.semaphore_signal(barrier, inc=1, device_id=peer("tm", off), device_id_type=MESH)
    for off in range(1, owner_count):
        pl.semaphore_signal(barrier, inc=1, device_id=peer("dm", off), device_id_type=MESH)
    pl.semaphore_wait(barrier, slabs + owner_count - 2)

    copies = []
    for off in range(1, slabs):
        copy = pltpu.make_async_remote_copy(
            src_ref=band_ref,
            dst_ref=bands.at[off - 1],
            send_sem=band_send.at[off - 1],
            recv_sem=band_recv.at[off - 1],
            device_id=peer("tm", off),
            device_id_type=MESH,
        )
        copy.start()
        copies.append(copy)
    tot[...] = jnp.zeros_like(tot)
    band = band_ref[...]
    for off in range(1, slabs):
        copies[off - 1].wait()
        band = band + bands[off - 1]
    inv[...] = 1.0 / (band * (1.0 / spectra) + 1e-06)

    even = lax.broadcasted_iota(jnp.int32, (FD * groups, SIDE), 1) % 2 == 0

    def block(step, carry):
        for s in range(0, SPB, 2):
            flats = []
            for k in (s, s + 1):
                start = pl.multiple_of((step * SPB + k) * SIDE, SIDE)
                ratio = p_ref[pl.ds(start, SIDE)] * inv[...]
                mean = jnp.sum(jnp.sum(ratio, 0, keepdims=True), 1, keepdims=True)
                flats.append((ratio - mean * (1.0 / (SIDE * SIDE))).astype(BF16))
            r = jnp.dot(m_ref[...], jnp.concatenate(flats, 1), preferred_element_type=F32)
            for m in range(2):
                part = r[:, m * SIDE : (m + 1) * SIDE]
                part = jnp.where(even, part[: FD * groups], part[FD * groups :])
                for d in range(FD):
                    tot[step * SPB + s + m + d] += part[d * groups : (d + 1) * groups]
        return carry

    blocks = spec // SPB
    last = -(-(halo + FD - 1) // SPB)
    lax.fori_loop(blocks - last, blocks, block, 0)
    if slabs > 1:
        tail_copy = pltpu.make_async_remote_copy(
            src_ref=tot.at[pl.ds(spec - halo, halo + FD - 1)],
            dst_ref=tail,
            send_sem=tail_send,
            recv_sem=tail_recv,
            device_id=peer("tm", 1),
            device_id_type=MESH,
        )
        tail_copy.start()
        lax.fori_loop(0, blocks - last, block, 0)
        tail_copy.wait()
        before = jnp.where(tm > 0, tail[...], 0.0)
    else:
        lax.fori_loop(0, blocks - last, block, 0)
        before = jnp.zeros(tail.shape, F32)

    rows = spec + halo + 1
    ext = jnp.concatenate(
        [
            jnp.zeros((1, groups, SIDE), F32),
            before[:halo],
            tot[: FD - 1] + before[halo:],
            tot[FD - 1 : spec],
        ],
        0,
    ).reshape(rows * groups, SIDE)
    width = SIDE * SIDE // NBLK
    sub = ((ext + pltpu.roll(ext, SIDE - 1, 1)) * (1.0 / math.sqrt(width))).astype(BF16)
    prod = jnp.dot(sub, mask_ref[...], preferred_element_type=F32)
    lanes = prod.shape[1]
    prod = prod.reshape(rows, groups, lanes)
    lane = lax.broadcasted_iota(jnp.int32, (groups, lanes), 1)
    row = lax.broadcasted_iota(jnp.int32, (groups, lanes), 0)
    own = (lane // 4) % groups == row
    each = jnp.sum(jnp.where(own[None], prod, 0.0), 1)
    count = spec + TT
    dd = 0.0
    for value in range(MAXT + 1):
        start = (MAXT - value) * TT
        dd = dd + each[start : start + count, value * quad : (value + 1) * quad]
    dd = dd * (1.0 / math.sqrt(NBLK))
    wide = pack_ref.shape[1]
    if quad < wide:
        dd = jnp.concatenate([dd, jnp.zeros((count, wide - quad), F32)], 1)
    dd = jnp.concatenate([dd, jnp.zeros((2 * SIDE - count, wide), F32)], 0)
    packed = jnp.dot(
        pack_ref[...], dd.T, preferred_element_type=F32, precision=lax.Precision.HIGHEST
    )
    send[...] = packed.reshape(send.shape)

    copies = []
    for off in range(1, owner_count):
        copy = pltpu.make_async_remote_copy(
            src_ref=send.at[lax.rem(dm + off, owner_count)],
            dst_ref=got.at[dm],
            send_sem=own_send.at[off - 1],
            recv_sem=own_recv.at[off - 1],
            device_id=peer("dm", off),
            device_id_type=MESH,
        )
        copy.start()
        copies.append(copy)
    got[dm] = send[dm]
    for copy in copies:
        copy.wait()

    slots, trials = out_ref.shape[0], out_ref.shape[2]
    for d in range(owner_count):
        part = got[d]
        acc = 0.0
        for lag in range(WMAX):
            moved = pltpu.roll(part, 2 * SIDE - (TT - lag), 1)[:, :SIDE]
            acc = acc + moved[:, None, :] * weight_ref[lag][None]
        for s in range(slots):
            out_ref[s, d] = acc[s * trials : (s + 1) * trials]


def search(power, band, mask, pack, widths, groups, capacity, trials, axes):
    slabs, owner_count = lax.axis_size("tm"), lax.axis_size("dm")
    spec = power.shape[0] // SIDE
    halo = MAXT * TT + WMAX - 1
    masks = fine_rows(groups, SIDE * SIDE // NBLK)
    lags = jnp.arange(WMAX, dtype=jnp.int32)
    weights = (lags[:, None] < widths[None, :]).astype(F32) / jnp.sqrt(widths.astype(F32))[None, :]
    weights = jnp.broadcast_to(weights[:, :, None], (WMAX, widths.shape[0], SIDE))
    sizes = (spec * slabs, spec, groups, slabs, owner_count, axes)
    block = pltpu.VMEM((owner_count, capacity * trials, 2 * SIDE), F32)
    sems = lambda n: pltpu.SemaphoreType.DMA((max(n, 1),))
    return pl.pallas_call(
        functools.partial(search_kernel, sizes),
        in_specs=[pl.BlockSpec(memory_space=pltpu.VMEM)] * 6,
        out_specs=pl.BlockSpec(memory_space=pltpu.VMEM),
        out_shape=jax.ShapeDtypeStruct(
            (capacity, owner_count, trials, widths.shape[0], spec), F32
        ),
        scratch_shapes=[
            pltpu.VMEM((max(slabs - 1, 1), SIDE, SIDE), F32),
            pltpu.VMEM((SIDE, SIDE), F32),
            pltpu.VMEM((spec + FD - 1, groups, SIDE), F32),
            pltpu.VMEM((halo + FD - 1, groups, SIDE), F32),
            block,
            block,
            sems(slabs - 1),
            sems(slabs - 1),
            pltpu.SemaphoreType.DMA,
            pltpu.SemaphoreType.DMA,
            sems(owner_count - 1),
            sems(owner_count - 1),
        ],
        compiler_params=pltpu.CompilerParams(
            vmem_limit_bytes=40 << 20, collective_id=0, has_side_effects=True
        ),
        name="search",
    )(power, band, masks, mask, pack, weights)


def slot_table(owners, owner_count, capacity):
    owner = owners[:, 0]
    index = jnp.arange(owner.shape[0], dtype=jnp.int32)
    same = owner[:, None] == owner[None, :]
    rank = jnp.sum((same & (index[None, :] < index[:, None])).astype(jnp.int32), 1)
    slot = owner * capacity + rank
    return slot[None, :] == jnp.arange(owner_count * capacity, dtype=jnp.int32)[:, None]


def shards(axes, raw, proto, delays, widths, owners):
    taps, channels = proto.shape
    spec = raw.shape[1] // channels
    groups, trials, _ = delays.shape
    owner_count = lax.axis_size("dm")
    capacity = 2 * (groups // owner_count)

    before = shifted(raw[:, raw.shape[1] - (taps - 1) * channels :], "tm", 1)
    power, band = front(raw, before, proto)

    value = jnp.arange(MAXT + 1, dtype=jnp.int32)[:, None, None, None]
    hit = (delays[None] == value).reshape(-1, NBLK).T
    mask = jnp.stack([hit, jnp.zeros_like(hit)], 1).reshape(SIDE, -1).astype(BF16)
    table = slot_table(owners, owner_count, capacity)
    pack = table[:, None, :, None] & jnp.eye(trials, dtype=bool)[None, :, None, :]
    pack = pack.reshape(owner_count * capacity * trials, groups * trials).astype(F32)
    pack = jnp.pad(pack, ((0, 0), (0, -pack.shape[1] % SIDE)))

    box = search(power, band, mask, pack, widths, groups, capacity, trials, axes)
    return box.astype(BF16)[:, :, None]


def solution(mesh):
    return jax.shard_map(
        functools.partial(shards, mesh.axis_names),
        mesh=mesh,
        in_specs=(P(("group", "dm", "beam"), "tm"), P(), P(), P(), P()),
        out_specs=P("dm", "group", "beam", None, None, "tm"),
        check_vma=False,
    )
```

```python
import functools
import math

import jax
import jax.numpy as jnp
import numpy as np
from jax import lax
from jax.experimental import pallas as pl
from jax.experimental.pallas import tpu as pltpu
from jax.sharding import PartitionSpec as P

SIDE = 128
NBLK = 64
FD = 4
TT = 8
MAXT = 3
WMAX = 8
SPB = 8
MESH = pl.DeviceIdType.MESH
F32 = jnp.float32
BF16 = jnp.bfloat16


def tables(channels):
    i = np.arange(SIDE)
    ang = (i[:, None] * i[None, :] % SIDE) * (2.0 * math.pi / SIDE)
    c, s = np.cos(ang), np.sin(ang)
    w1 = np.concatenate([c, s], 0)
    w2 = np.block([[c, -s], [-s, -c]])
    tw = (i[:, None] * i[None, :] % channels) * (2.0 * math.pi / channels)
    twiddle = np.stack([np.cos(tw), np.sin(tw)]).astype(np.float32)
    return jnp.asarray(w1, BF16), jnp.asarray(w2, BF16), jnp.asarray(twiddle)


def fine_rows(groups, width):
    g = np.arange(groups)[:, None]
    i = np.arange(width)[None, :]
    fine = g * FD * (width - 1 - i) // (groups * (width - 1))
    hot = np.stack([fine == step for step in range(FD)])
    hot = hot.reshape(FD, groups, width // SIDE, SIDE).transpose(2, 0, 1, 3)
    return jnp.asarray(hot.reshape(-1, SIDE), BF16)


def search_kernel(
    sizes, x_ref, raw_ref, proto_ref, w1_ref, w2_ref, tw_ref, m_ref, delays_ref, widths_ref, owners_ref, out_ref,
    window, early, history, filt, p_ref, band_ref, bands, inv, tot, tail, send, got,
    hist_send, hist_recv, band_send, band_recv, tail_send, tail_recv, own_send, own_recv,
):
    spectra, spec, groups, slabs, owner_count, axes = sizes
    step = pl.program_id(0)
    scale = 1.0 / (4 * SIDE * SIDE)
    frame_size = SIDE * SIDE
    tm = lax.axis_index("tm")

    def peer(axis, shift):
        place = {name: lax.axis_index(name) for name in axes}
        place[axis] = lax.rem(place[axis] + shift, lax.axis_size(axis))
        return tuple(place[name] for name in axes)

    def history_copy():
        size = history.shape[1]
        return pltpu.make_async_remote_copy(
            src_ref=raw_ref.at[:, pl.ds(spec * frame_size - size, size)],
            dst_ref=history,
            send_sem=hist_send,
            recv_sem=hist_recv,
            device_id=peer("tm", 1),
            device_id_type=MESH,
        )

    def unfold(ref, index):
        line = ref[:, index * frame_size : (index + 1) * frame_size]
        return line.astype(F32).reshape(SIDE, SIDE)

    def pair(win, s, start):
        ys = []
        for k in (s, s + 1):
            acc = win[k * SIDE : (k + 1) * SIDE] * filt[0]
            for tap in range(1, 4):
                acc = acc + win[(k + tap) * SIDE : (k + tap + 1) * SIDE] * filt[tap]
            ys.append(acc.astype(BF16))
        a = jnp.dot(w1_ref[...], jnp.concatenate(ys, 1), preferred_element_type=F32)
        ts = []
        for m in range(2):
            re = a[:SIDE, m * SIDE : (m + 1) * SIDE]
            im = a[SIDE:, m * SIDE : (m + 1) * SIDE]
            t_re = re * tw_ref[0] - im * tw_ref[1]
            t_ni = im * tw_ref[0] + re * tw_ref[1]
            ts.append(jnp.concatenate([t_re.astype(BF16), t_ni.astype(BF16)], 1))
        c = jnp.dot(jnp.concatenate(ts, 0), w2_ref[...], preferred_element_type=F32)
        re, im = c[:, :SIDE], c[:, SIDE:]
        power = (re * re + im * im) * scale
        p_ref[pl.ds(start, 2 * SIDE)] = power
        band_ref[...] += power[:SIDE] + power[SIDE:]

    @pl.when(step == 0)
    def _():
        barrier = pltpu.get_barrier_semaphore()
        for off in range(1, slabs):
            pl.semaphore_signal(barrier, inc=1, device_id=peer("tm", off), device_id_type=MESH)
        for off in range(1, owner_count):
            pl.semaphore_signal(barrier, inc=1, device_id=peer("dm", off), device_id_type=MESH)
        pl.semaphore_wait(barrier, slabs + owner_count - 2)
        if slabs > 1:
            history_copy().start()
        for tap in range(4):
            filt[tap] = unfold(proto_ref.at[tap : tap + 1], 0)
        band_ref[...] = jnp.zeros_like(band_ref)
        tot[...] = jnp.zeros_like(tot)
        for k in range(4):
            early[(k + 3) * SIDE : (k + 4) * SIDE] = unfold(x_ref, k)

    @pl.when(step > 0)
    def _():
        for k in range(4):
            window[(k + 3) * SIDE : (k + 4) * SIDE] = unfold(x_ref, k)
        for s in (0, 2):
            pair(window, s, pl.multiple_of((step * SPB + s) * SIDE, SIDE))

    @pl.when(step == 0)
    def _():
        window[4 * SIDE : 7 * SIDE] = early[4 * SIDE : 7 * SIDE]

    for k in range(4, SPB):
        window[(k + 3) * SIDE : (k + 4) * SIDE] = unfold(x_ref, k)
    for s in range(4, SPB, 2):
        pair(window, s, pl.multiple_of((step * SPB + s) * SIDE, SIDE))
    window[: 3 * SIDE] = window[SPB * SIDE :]

    @pl.when(step == spec // SPB - 1)
    def _():
        if slabs > 1:
            history_copy().wait()
            for k in range(3):
                early[k * SIDE : (k + 1) * SIDE] = jnp.where(tm > 0, unfold(history, k), 0.0)
        else:
            early[: 3 * SIDE] = jnp.zeros((3 * SIDE, SIDE), F32)
        for s in (0, 2):
            pair(early, s, s * SIDE)
        finish(
            sizes, peer, m_ref, delays_ref, widths_ref, owners_ref, out_ref,
            p_ref, band_ref, bands, inv, tot, tail, send, got,
            band_send, band_recv, tail_send, tail_recv, own_send, own_recv,
        )


def finish(
    sizes, peer, m_ref, delays_ref, widths_ref, owners_ref, out_ref,
    p_ref, band_ref, bands, inv, tot, tail, send, got,
    band_send, band_recv, tail_send, tail_recv, own_send, own_recv,
):
    spectra, spec, groups, slabs, owner_count, axes = sizes
    halo = MAXT * TT + WMAX - 1
    slots, trials = out_ref.shape[0], out_ref.shape[2]
    quad = trials * groups
    tm, dm = lax.axis_index("tm"), lax.axis_index("dm")

    copies = []
    for off in range(1, slabs):
        copy = pltpu.make_async_remote_copy(
            src_ref=band_ref,
            dst_ref=bands.at[off - 1],
            send_sem=band_send.at[off - 1],
            recv_sem=band_recv.at[off - 1],
            device_id=peer("tm", off),
            device_id_type=MESH,
        )
        copy.start()
        copies.append(copy)
    iota = lambda shape, dim: lax.broadcasted_iota(jnp.int32, shape, dim)
    spread = (iota((NBLK, SIDE), 1) == 2 * iota((NBLK, SIDE), 0)).astype(BF16)
    late = jnp.dot(delays_ref[...].astype(F32).astype(BF16), spread, preferred_element_type=F32)
    on = iota((quad, SIDE), 1) % 2 == 0
    mask = jnp.concatenate(
        [jnp.where(on & (late == float(v)), 1.0, 0.0) for v in range(MAXT + 1)], 0
    ).astype(BF16)
    wide = max(SIDE, quad)
    lane = iota((groups, wide), 1)
    row = iota((groups, wide), 0)
    owner = jnp.broadcast_to(owners_ref[...], (groups, wide))
    mine = jnp.sum(jnp.where(lane // trials == row, owner, 0), 0, keepdims=True)
    rank = jnp.sum(jnp.where((owner == mine) & (row < lane // trials), 1, 0), 0, keepdims=True)
    place = (mine * slots + rank) * trials + lane[:1] % trials
    place = jnp.where(lane[:1] < quad, place, -1)
    rows_out = owner_count * slots * trials
    pack = jnp.where(iota((rows_out, wide), 0) == place, 1.0, 0.0)
    reach = jnp.broadcast_to(widths_ref[...], (widths_ref.shape[0], SIDE))
    root = 1.0 / jnp.sqrt(reach.astype(F32))
    weights = [jnp.where(reach > lag, root, 0.0) for lag in range(WMAX)]

    band = band_ref[...]
    for off in range(1, slabs):
        copies[off - 1].wait()
        band = band + bands[off - 1]
    inv[...] = 1.0 / (band * (1.0 / spectra) + 1e-06)

    even = lax.broadcasted_iota(jnp.int32, (FD * groups, SIDE), 1) % 2 == 0

    def block(step, carry):
        for s in range(0, SPB, 2):
            flats = []
            for k in (s, s + 1):
                start = pl.multiple_of((step * SPB + k) * SIDE, SIDE)
                ratio = p_ref[pl.ds(start, SIDE)] * inv[...]
                mean = jnp.sum(jnp.sum(ratio, 0, keepdims=True), 1, keepdims=True)
                flats.append((ratio - mean * (1.0 / (SIDE * SIDE))).astype(BF16))
            r = jnp.dot(m_ref[...], jnp.concatenate(flats, 1), preferred_element_type=F32)
            for m in range(2):
                part = r[:, m * SIDE : (m + 1) * SIDE]
                part = jnp.where(even, part[: FD * groups], part[FD * groups :])
                for d in range(FD):
                    tot[step * SPB + s + m + d] += part[d * groups : (d + 1) * groups]
        return carry

    blocks = spec // SPB
    last = -(-(halo + FD - 1) // SPB)
    lax.fori_loop(blocks - last, blocks, block, 0)
    if slabs > 1:
        tail_copy = pltpu.make_async_remote_copy(
            src_ref=tot.at[pl.ds(spec - halo, halo + FD - 1)],
            dst_ref=tail,
            send_sem=tail_send,
            recv_sem=tail_recv,
            device_id=peer("tm", 1),
            device_id_type=MESH,
        )
        tail_copy.start()
        lax.fori_loop(0, blocks - last, block, 0)
        tail_copy.wait()
        before = jnp.where(tm > 0, tail[...], 0.0)
    else:
        lax.fori_loop(0, blocks - last, block, 0)
        before = jnp.zeros(tail.shape, F32)

    rows = spec + halo + 1
    ext = jnp.concatenate(
        [
            jnp.zeros((1, groups, SIDE), F32),
            before[:halo],
            tot[: FD - 1] + before[halo:],
            tot[FD - 1 : spec],
        ],
        0,
    ).reshape(rows * groups, SIDE)
    width = SIDE * SIDE // NBLK
    sub = ((ext + pltpu.roll(ext, SIDE - 1, 1)) * (1.0 / math.sqrt(width))).astype(BF16)
    prod = lax.dot_general(
        sub, mask, (((1,), (1,)), ((), ())), preferred_element_type=F32
    )
    lanes = prod.shape[1]
    prod = prod.reshape(rows, groups, lanes)
    lane = lax.broadcasted_iota(jnp.int32, (groups, lanes), 1)
    row = lax.broadcasted_iota(jnp.int32, (groups, lanes), 0)
    own = (lane // trials) % groups == row
    each = jnp.sum(jnp.where(own[None], prod, 0.0), 1)
    count = spec + TT
    dd = 0.0
    for value in range(MAXT + 1):
        start = (MAXT - value) * TT
        dd = dd + each[start : start + count, value * quad : (value + 1) * quad]
    dd = dd * (1.0 / math.sqrt(NBLK))
    if quad < wide:
        dd = jnp.concatenate([dd, jnp.zeros((count, wide - quad), F32)], 1)
    dd = jnp.concatenate([dd, jnp.zeros((2 * SIDE - count, wide), F32)], 0)
    packed = jnp.dot(
        pack, dd.T, preferred_element_type=F32, precision=lax.Precision.HIGHEST
    )
    send[...] = packed.reshape(send.shape)

    copies = []
    for off in range(1, owner_count):
        copy = pltpu.make_async_remote_copy(
            src_ref=send.at[lax.rem(dm + off, owner_count)],
            dst_ref=got.at[dm],
            send_sem=own_send.at[off - 1],
            recv_sem=own_recv.at[off - 1],
            device_id=peer("dm", off),
            device_id_type=MESH,
        )
        copy.start()
        copies.append(copy)
    got[dm] = send[dm]
    for copy in copies:
        copy.wait()

    for d in range(owner_count):
        part = got[d]
        acc = 0.0
        for lag in range(WMAX):
            moved = pltpu.roll(part, 2 * SIDE - (TT - lag), 1)[:, :SIDE]
            acc = acc + moved[:, None, :] * weights[lag][None]
        for s in range(slots):
            out_ref[s, d] = acc[s * trials : (s + 1) * trials]


def shards(axes, raw, proto, delays, widths, owners):
    taps, channels = proto.shape
    spec = raw.shape[1] // channels
    groups, trials, _ = delays.shape
    slabs, owner_count = lax.axis_size("tm"), lax.axis_size("dm")
    capacity = 2 * (groups // owner_count)
    halo = MAXT * TT + WMAX - 1
    w1, w2, tw = tables(channels)
    masks = fine_rows(groups, channels // NBLK)
    sizes = (spec * slabs, spec, groups, slabs, owner_count, axes)
    block = pltpu.VMEM((owner_count, capacity * trials, 2 * SIDE), F32)
    sems = lambda n: pltpu.SemaphoreType.DMA((max(n, 1),))
    full = lambda shape: pl.BlockSpec(shape, lambda i: (0,) * len(shape))
    small = [proto, w1, w2, tw, masks, delays.reshape(groups * trials, NBLK), widths[:, None], owners]
    out = (capacity, owner_count, trials, widths.shape[0], spec)
    box = pl.pallas_call(
        functools.partial(search_kernel, sizes),
        grid=(spec // SPB,),
        in_specs=[
            pl.BlockSpec((1, SPB * channels), lambda i: (0, i)),
            pl.BlockSpec(memory_space=pl.ANY),
            *[full(value.shape) for value in small],
        ],
        out_specs=full(out),
        out_shape=jax.ShapeDtypeStruct(out, F32),
        scratch_shapes=[
            pltpu.VMEM(((SPB + 3) * SIDE, SIDE), F32),
            pltpu.VMEM((7 * SIDE, SIDE), F32),
            pltpu.VMEM((1, 3 * channels), BF16),
            pltpu.VMEM((taps, SIDE, SIDE), F32),
            pltpu.VMEM((spec * SIDE, SIDE), F32),
            pltpu.VMEM((SIDE, SIDE), F32),
            pltpu.VMEM((max(slabs - 1, 1), SIDE, SIDE), F32),
            pltpu.VMEM((SIDE, SIDE), F32),
            pltpu.VMEM((spec + FD - 1, groups, SIDE), F32),
            pltpu.VMEM((halo + FD - 1, groups, SIDE), F32),
            block,
            block,
            pltpu.SemaphoreType.DMA,
            pltpu.SemaphoreType.DMA,
            sems(slabs - 1),
            sems(slabs - 1),
            pltpu.SemaphoreType.DMA,
            pltpu.SemaphoreType.DMA,
            sems(owner_count - 1),
            sems(owner_count - 1),
        ],
        compiler_params=pltpu.CompilerParams(
            vmem_limit_bytes=56 << 20, collective_id=0, has_side_effects=True
        ),
        name="search",
    )(raw, raw, *small)
    return box.astype(BF16)[:, :, None]


def solution(mesh):
    return jax.shard_map(
        functools.partial(shards, mesh.axis_names),
        mesh=mesh,
        in_specs=(P(("group", "dm", "beam"), "tm"), P(), P(), P(), P()),
        out_specs=P("dm", "group", "beam", None, None, "tm"),
        check_vma=False,
    )
```

```python
import functools
import math

import jax
import jax.numpy as jnp
import numpy as np
from jax import lax
from jax.experimental import pallas as pl
from jax.experimental.pallas import tpu as pltpu
from jax.sharding import PartitionSpec as P

SIDE = 128
NBLK = 64
FD = 4
TT = 8
MAXT = 3
WMAX = 8
SPB = 8
HALF = SIDE // 2
FR = 80
MESH = pl.DeviceIdType.MESH
F32 = jnp.float32
BF16 = jnp.bfloat16


def tables(channels):
    i = np.arange(SIDE)
    ang = (i[:, None] * i[None, :] % SIDE) * (2.0 * math.pi / SIDE)
    c, s = np.cos(ang), np.sin(ang)
    w1 = np.concatenate([c[:FR], s[:FR]], 0)
    w2 = np.block([[c, -s], [-s, -c]])
    tw = (i[:, None] * i[None, :] % channels) * (2.0 * math.pi / channels)
    twiddle = np.stack([np.cos(tw[:FR]), np.sin(tw[:FR])]).astype(np.float32)
    return jnp.asarray(w1, BF16), jnp.asarray(w2, BF16), jnp.asarray(twiddle)


def fine_rows(groups, width):
    g = np.arange(groups)[:, None]
    i = np.arange(width)[None, :]
    fine = g * FD * (width - 1 - i) // (groups * (width - 1))
    hot = np.stack([fine == step for step in range(FD)])
    hot = hot.reshape(FD, groups, width // SIDE, SIDE).transpose(2, 0, 1, 3)
    out = np.zeros((2, 2, FD, groups, FR))
    out[0, ..., : HALF + 1] = hot[..., : HALF + 1]
    out[1, ..., 1:HALF] = hot[..., : HALF : -1]
    return jnp.asarray(out.reshape(-1, FR), BF16)


def search_kernel(
    sizes, x_ref, raw_ref, proto_ref, w1_ref, w2_ref, tw_ref, m_ref, delays_ref, widths_ref, owners_ref, out_ref,
    window, early, history, filt, p_ref, band_ref, bands, inv, direct, mirror, tot, tail, send, got,
    hist_send, hist_recv, band_send, band_recv, tail_send, tail_recv, own_send, own_recv,
):
    spectra, spec, groups, slabs, owner_count, axes = sizes
    step = pl.program_id(0)
    scale = 1.0 / (4 * SIDE * SIDE)
    frame_size = SIDE * SIDE
    tm = lax.axis_index("tm")

    def peer(axis, shift):
        place = {name: lax.axis_index(name) for name in axes}
        place[axis] = lax.rem(place[axis] + shift, lax.axis_size(axis))
        return tuple(place[name] for name in axes)

    def history_copy():
        size = history.shape[1]
        return pltpu.make_async_remote_copy(
            src_ref=raw_ref.at[:, pl.ds(spec * frame_size - size, size)],
            dst_ref=history,
            send_sem=hist_send,
            recv_sem=hist_recv,
            device_id=peer("tm", 1),
            device_id_type=MESH,
        )

    def unfold(ref, index):
        line = ref[:, index * frame_size : (index + 1) * frame_size]
        return line.astype(F32).reshape(SIDE, SIDE)

    def pair(win, s, start):
        ys = []
        for k in (s, s + 1):
            acc = win[k * SIDE : (k + 1) * SIDE] * filt[0]
            for tap in range(1, 4):
                acc = acc + win[(k + tap) * SIDE : (k + tap + 1) * SIDE] * filt[tap]
            ys.append(acc.astype(BF16))
        a = jnp.dot(w1_ref[...], jnp.concatenate(ys, 1), preferred_element_type=F32)
        ts = []
        for m in range(2):
            re = a[:FR, m * SIDE : (m + 1) * SIDE]
            im = a[FR:, m * SIDE : (m + 1) * SIDE]
            t_re = re * tw_ref[0] - im * tw_ref[1]
            t_ni = im * tw_ref[0] + re * tw_ref[1]
            ts.append(jnp.concatenate([t_re.astype(BF16), t_ni.astype(BF16)], 1))
        c = jnp.dot(jnp.concatenate(ts, 0), w2_ref[...], preferred_element_type=F32)
        re, im = c[:, :SIDE], c[:, SIDE:]
        power = (re * re + im * im) * scale
        p_ref[pl.ds(start, 2 * FR)] = power
        band_ref[...] += power[:FR] + power[FR:]

    @pl.when(step == 0)
    def _():
        barrier = pltpu.get_barrier_semaphore()
        for off in range(1, slabs):
            pl.semaphore_signal(barrier, inc=1, device_id=peer("tm", off), device_id_type=MESH)
        for off in range(1, owner_count):
            pl.semaphore_signal(barrier, inc=1, device_id=peer("dm", off), device_id_type=MESH)
        pl.semaphore_wait(barrier, slabs + owner_count - 2)
        if slabs > 1:
            history_copy().start()
        for tap in range(4):
            filt[tap] = unfold(proto_ref.at[tap : tap + 1], 0)
        band_ref[...] = jnp.zeros_like(band_ref)
        direct[...] = jnp.zeros_like(direct)
        mirror[...] = jnp.zeros_like(mirror)
        for k in range(4):
            early[(k + 3) * SIDE : (k + 4) * SIDE] = unfold(x_ref, k)

    @pl.when(step > 0)
    def _():
        for k in range(4):
            window[(k + 3) * SIDE : (k + 4) * SIDE] = unfold(x_ref, k)
        for s in (0, 2):
            pair(window, s, pl.multiple_of((step * SPB + s) * FR, FR))

    @pl.when(step == 0)
    def _():
        window[4 * SIDE : 7 * SIDE] = early[4 * SIDE : 7 * SIDE]

    for k in range(4, SPB):
        window[(k + 3) * SIDE : (k + 4) * SIDE] = unfold(x_ref, k)
    for s in range(4, SPB, 2):
        pair(window, s, pl.multiple_of((step * SPB + s) * FR, FR))
    window[: 3 * SIDE] = window[SPB * SIDE :]

    @pl.when(step == spec // SPB - 1)
    def _():
        if slabs > 1:
            history_copy().wait()
            for k in range(3):
                early[k * SIDE : (k + 1) * SIDE] = jnp.where(tm > 0, unfold(history, k), 0.0)
        else:
            early[: 3 * SIDE] = jnp.zeros((3 * SIDE, SIDE), F32)
        for s in (0, 2):
            pair(early, s, s * FR)
        finish(
            sizes, peer, m_ref, delays_ref, widths_ref, owners_ref, out_ref,
            p_ref, band_ref, bands, inv, direct, mirror, tot, tail, send, got,
            band_send, band_recv, tail_send, tail_recv, own_send, own_recv,
        )


def finish(
    sizes, peer, m_ref, delays_ref, widths_ref, owners_ref, out_ref,
    p_ref, band_ref, bands, inv, direct, mirror, tot, tail, send, got,
    band_send, band_recv, tail_send, tail_recv, own_send, own_recv,
):
    spectra, spec, groups, slabs, owner_count, axes = sizes
    halo = MAXT * TT + WMAX - 1
    slots, trials = out_ref.shape[0], out_ref.shape[2]
    quad = trials * groups
    tm, dm = lax.axis_index("tm"), lax.axis_index("dm")

    copies = []
    for off in range(1, slabs):
        copy = pltpu.make_async_remote_copy(
            src_ref=band_ref,
            dst_ref=bands.at[off - 1],
            send_sem=band_send.at[off - 1],
            recv_sem=band_recv.at[off - 1],
            device_id=peer("tm", off),
            device_id_type=MESH,
        )
        copy.start()
        copies.append(copy)
    iota = lambda shape, dim: lax.broadcasted_iota(jnp.int32, shape, dim)
    spread = (iota((NBLK, SIDE), 1) == 2 * iota((NBLK, SIDE), 0)).astype(BF16)
    late = jnp.dot(delays_ref[...].astype(F32).astype(BF16), spread, preferred_element_type=F32)
    on = iota((quad, SIDE), 1) % 2 == 0
    mask = jnp.concatenate(
        [jnp.where(on & (late == float(v)), 1.0, 0.0) for v in range(MAXT + 1)], 0
    ).astype(BF16)
    def column(ref):
        n = ref.shape[1]
        same = iota((n, n), 0) == iota((n, n), 1)
        return jnp.sum(jnp.where(same, jnp.broadcast_to(ref[...], (n, n)), 0), 1, keepdims=True)

    wide = max(SIDE, quad)
    lane = iota((groups, wide), 1)
    row = iota((groups, wide), 0)
    owner = jnp.broadcast_to(column(owners_ref), (groups, wide))
    mine = jnp.sum(jnp.where(lane // trials == row, owner, 0), 0, keepdims=True)
    rank = jnp.sum(jnp.where((owner == mine) & (row < lane // trials), 1, 0), 0, keepdims=True)
    place = (mine * slots + rank) * trials + lane[:1] % trials
    place = jnp.where(lane[:1] < quad, place, -1)
    rows_out = owner_count * slots * trials
    pack = jnp.where(iota((rows_out, wide), 0) == place, 1.0, 0.0)
    reach = jnp.broadcast_to(column(widths_ref), (widths_ref.shape[1], SIDE))
    root = 1.0 / jnp.sqrt(reach.astype(F32))
    weights = [jnp.where(reach > lag, root, 0.0) for lag in range(WMAX)]

    band = band_ref[...]
    for off in range(1, slabs):
        copies[off - 1].wait()
        band = band + bands[off - 1]
    held = lax.broadcasted_iota(jnp.int32, (FR, SIDE), 0) <= HALF
    inv[...] = jnp.where(held, 1.0 / (band * (1.0 / spectra) + 1e-06), 0.0)

    even = lax.broadcasted_iota(jnp.int32, (FD * groups, SIDE), 1) % 2 == 0

    def block(step, carry):
        for s in range(0, SPB, 2):
            flats = []
            for k in (s, s + 1):
                start = pl.multiple_of((step * SPB + k) * FR, FR)
                ratio = p_ref[pl.ds(start, FR)] * inv[...]
                line = 2.0 * jnp.sum(ratio, 0, keepdims=True) - ratio[:1] - ratio[HALF : HALF + 1]
                mean = jnp.sum(line, 1, keepdims=True) * (1.0 / (SIDE * SIDE))
                flats.append((ratio - mean).astype(BF16))
            r = jnp.dot(m_ref[...], jnp.concatenate(flats, 1), preferred_element_type=F32)
            size = FD * groups
            for m in range(2):
                part = r[:, m * SIDE : (m + 1) * SIDE]
                one = jnp.where(even, part[:size], part[size : 2 * size])
                two = jnp.where(even, part[3 * size :], part[2 * size : 3 * size])
                for d in range(FD):
                    direct[step * SPB + s + m + d] += one[d * groups : (d + 1) * groups]
                    mirror[step * SPB + s + m + d] += two[d * groups : (d + 1) * groups]
        return carry

    def combine(first, stop):
        one = direct[first:stop].reshape(-1, SIDE)
        two = mirror[first:stop].reshape(-1, SIDE)
        high = two.astype(BF16)
        low = (two - high.astype(F32)).astype(BF16)
        both = jnp.concatenate([high, low], 1)
        turned = jnp.dot(both, turn, preferred_element_type=F32)
        total = one + pltpu.roll(one, SIDE - 1, 1) + turned
        tot[first:stop] = total.reshape(stop - first, groups, SIDE)

    source = iota((2 * SIDE, SIDE), 0) % SIDE
    goal = iota((2 * SIDE, SIDE), 1)
    turn = jnp.where((goal % 2 == 0) & (source // 2 == HALF - 1 - goal // 2), 1.0, 0.0).astype(BF16)
    blocks = spec // SPB
    last = -(-(halo + FD - 1) // SPB)
    lax.fori_loop(blocks - last, blocks, block, 0)
    combine(spec - halo, spec + FD - 1)
    if slabs > 1:
        tail_copy = pltpu.make_async_remote_copy(
            src_ref=tot.at[pl.ds(spec - halo, halo + FD - 1)],
            dst_ref=tail,
            send_sem=tail_send,
            recv_sem=tail_recv,
            device_id=peer("tm", 1),
            device_id_type=MESH,
        )
        tail_copy.start()
        lax.fori_loop(0, blocks - last, block, 0)
        combine(0, spec - halo)
        tail_copy.wait()
        before = jnp.where(tm > 0, tail[...], 0.0)
    else:
        lax.fori_loop(0, blocks - last, block, 0)
        combine(0, spec - halo)
        before = jnp.zeros(tail.shape, F32)

    rows = spec + halo + 1
    ext = jnp.concatenate(
        [
            jnp.zeros((1, groups, SIDE), F32),
            before[:halo],
            tot[: FD - 1] + before[halo:],
            tot[FD - 1 : spec],
        ],
        0,
    ).reshape(rows * groups, SIDE)
    width = SIDE * SIDE // NBLK
    sub = (ext * (1.0 / math.sqrt(width))).astype(BF16)
    prod = lax.dot_general(
        sub, mask, (((1,), (1,)), ((), ())), preferred_element_type=F32
    )
    lanes = prod.shape[1]
    prod = prod.reshape(rows, groups, lanes)
    lane = lax.broadcasted_iota(jnp.int32, (groups, lanes), 1)
    row = lax.broadcasted_iota(jnp.int32, (groups, lanes), 0)
    own = (lane // trials) % groups == row
    each = jnp.sum(jnp.where(own[None], prod, 0.0), 1)
    count = spec + TT
    dd = 0.0
    for value in range(MAXT + 1):
        start = (MAXT - value) * TT
        dd = dd + each[start : start + count, value * quad : (value + 1) * quad]
    dd = dd * (1.0 / math.sqrt(NBLK))
    if quad < wide:
        dd = jnp.concatenate([dd, jnp.zeros((count, wide - quad), F32)], 1)
    dd = jnp.concatenate([dd, jnp.zeros((2 * SIDE - count, wide), F32)], 0)
    packed = jnp.dot(
        pack, dd.T, preferred_element_type=F32, precision=lax.Precision.HIGHEST
    )
    send[...] = packed.reshape(send.shape)

    copies = []
    for off in range(1, owner_count):
        copy = pltpu.make_async_remote_copy(
            src_ref=send.at[lax.rem(dm + off, owner_count)],
            dst_ref=got.at[dm],
            send_sem=own_send.at[off - 1],
            recv_sem=own_recv.at[off - 1],
            device_id=peer("dm", off),
            device_id_type=MESH,
        )
        copy.start()
        copies.append(copy)
    got[dm] = send[dm]
    for copy in copies:
        copy.wait()

    for d in range(owner_count):
        part = got[d]
        acc = 0.0
        for lag in range(WMAX):
            moved = pltpu.roll(part, 2 * SIDE - (TT - lag), 1)[:, :SIDE]
            acc = acc + moved[:, None, :] * weights[lag][None]
        for s in range(slots):
            out_ref[s, d] = acc[s * trials : (s + 1) * trials]


def shards(axes, raw, proto, delays, widths, owners):
    taps, channels = proto.shape
    spec = raw.shape[1] // channels
    groups, trials, _ = delays.shape
    slabs, owner_count = lax.axis_size("tm"), lax.axis_size("dm")
    capacity = 2 * (groups // owner_count)
    halo = MAXT * TT + WMAX - 1
    w1, w2, tw = tables(channels)
    masks = fine_rows(groups, channels // NBLK)
    sizes = (spec * slabs, spec, groups, slabs, owner_count, axes)
    block = pltpu.VMEM((owner_count, capacity * trials, 2 * SIDE), F32)
    sems = lambda n: pltpu.SemaphoreType.DMA((max(n, 1),))
    full = lambda shape: pl.BlockSpec(shape, lambda i: (0,) * len(shape))
    small = [proto, w1, w2, tw, masks, delays.reshape(groups * trials, NBLK), widths[None], owners.T]
    out = (capacity, owner_count, trials, widths.shape[0], spec)
    box = pl.pallas_call(
        functools.partial(search_kernel, sizes),
        grid=(spec // SPB,),
        in_specs=[
            pl.BlockSpec((1, SPB * channels), lambda i: (0, i)),
            pl.BlockSpec(memory_space=pl.ANY),
            *[full(value.shape) for value in small],
        ],
        out_specs=full(out),
        out_shape=jax.ShapeDtypeStruct(out, F32),
        scratch_shapes=[
            pltpu.VMEM(((SPB + 3) * SIDE, SIDE), F32),
            pltpu.VMEM((7 * SIDE, SIDE), F32),
            pltpu.VMEM((1, 3 * channels), BF16),
            pltpu.VMEM((taps, SIDE, SIDE), F32),
            pltpu.VMEM((spec * FR, SIDE), F32),
            pltpu.VMEM((FR, SIDE), F32),
            pltpu.VMEM((max(slabs - 1, 1), FR, SIDE), F32),
            pltpu.VMEM((FR, SIDE), F32),
            pltpu.VMEM((spec + FD - 1, groups, SIDE), F32),
            pltpu.VMEM((spec + FD - 1, groups, SIDE), F32),
            pltpu.VMEM((spec + FD - 1, groups, SIDE), F32),
            pltpu.VMEM((halo + FD - 1, groups, SIDE), F32),
            block,
            block,
            pltpu.SemaphoreType.DMA,
            pltpu.SemaphoreType.DMA,
            sems(slabs - 1),
            sems(slabs - 1),
            pltpu.SemaphoreType.DMA,
            pltpu.SemaphoreType.DMA,
            sems(owner_count - 1),
            sems(owner_count - 1),
        ],
        compiler_params=pltpu.CompilerParams(
            vmem_limit_bytes=56 << 20, collective_id=0, has_side_effects=True
        ),
        name="search",
    )(raw, raw, *small)
    return box.astype(BF16)[:, :, None]


def solution(mesh):
    return jax.shard_map(
        functools.partial(shards, mesh.axis_names),
        mesh=mesh,
        in_specs=(P(("group", "dm", "beam"), "tm"), P(), P(), P(), P()),
        out_specs=P("dm", "group", "beam", None, None, "tm"),
        check_vma=False,
    )
```

```python
import functools
import math

import jax
import jax.numpy as jnp
import numpy as np
from jax import lax
from jax.experimental import pallas as pl
from jax.experimental.pallas import tpu as pltpu
from jax.sharding import PartitionSpec as P

SIDE = 128
NBLK = 64
FD = 4
TT = 8
MAXT = 3
WMAX = 8
SPB = 32
HALF = SIDE // 2
FR = 80
MESH = pl.DeviceIdType.MESH
F32 = jnp.float32
BF16 = jnp.bfloat16


def tables(channels):
    i = np.arange(SIDE)
    ang = (i[:, None] * i[None, :] % SIDE) * (2.0 * math.pi / SIDE)
    c, s = np.cos(ang), np.sin(ang)
    w1 = np.concatenate([c[:FR], s[:FR]], 0)
    w2 = np.block([[c, -s], [-s, -c]])
    tw = (i[:, None] * i[None, :] % channels) * (2.0 * math.pi / channels)
    twiddle = np.stack([np.cos(tw[:FR]), np.sin(tw[:FR])]).astype(np.float32)
    return jnp.asarray(w1, BF16), jnp.asarray(w2, BF16), jnp.asarray(twiddle)


def fine_rows(groups, width):
    g = np.arange(groups)[:, None]
    i = np.arange(width)[None, :]
    fine = g * FD * (width - 1 - i) // (groups * (width - 1))
    hot = np.stack([fine == step for step in range(FD)])
    hot = hot.reshape(FD, groups, width // SIDE, SIDE).transpose(2, 0, 1, 3)
    out = np.zeros((2, 2, FD, groups, FR))
    out[0, ..., : HALF + 1] = hot[..., : HALF + 1]
    out[1, ..., 1:HALF] = hot[..., : HALF : -1]
    return jnp.asarray(out.reshape(-1, FR), BF16)


def search_kernel(
    sizes, x_ref, raw_ref, proto_ref, w1_ref, w2_ref, tw_ref, m_ref, delays_ref, widths_ref, owners_ref, out_ref,
    window, early, history, filt, p_ref, band_ref, bands, inv, direct, mirror, tot, tail, send, got,
    hist_send, hist_recv, band_send, band_recv, tail_send, tail_recv, own_send, own_recv,
):
    spectra, spec, groups, slabs, owner_count, axes = sizes
    step = pl.program_id(0)
    scale = 1.0 / (4 * SIDE * SIDE)
    frame_size = SIDE * SIDE
    tm = lax.axis_index("tm")

    def peer(axis, shift):
        place = {name: lax.axis_index(name) for name in axes}
        place[axis] = lax.rem(place[axis] + shift, lax.axis_size(axis))
        return tuple(place[name] for name in axes)

    def history_copy():
        size = history.shape[1]
        return pltpu.make_async_remote_copy(
            src_ref=raw_ref.at[:, pl.ds(spec * frame_size - size, size)],
            dst_ref=history,
            send_sem=hist_send,
            recv_sem=hist_recv,
            device_id=peer("tm", 1),
            device_id_type=MESH,
        )

    def unfold(ref, index):
        line = ref[:, index * frame_size : (index + 1) * frame_size]
        return line.astype(F32).reshape(SIDE, SIDE)

    def pair(win, s, start):
        ys = []
        for k in (s, s + 1):
            acc = win[k * SIDE : (k + 1) * SIDE] * filt[0]
            for tap in range(1, 4):
                acc = acc + win[(k + tap) * SIDE : (k + tap + 1) * SIDE] * filt[tap]
            ys.append(acc.astype(BF16))
        a = jnp.dot(w1_ref[...], jnp.concatenate(ys, 1), preferred_element_type=F32)
        ts = []
        for m in range(2):
            re = a[:FR, m * SIDE : (m + 1) * SIDE]
            im = a[FR:, m * SIDE : (m + 1) * SIDE]
            t_re = re * tw_ref[0] - im * tw_ref[1]
            t_ni = im * tw_ref[0] + re * tw_ref[1]
            ts.append(jnp.concatenate([t_re.astype(BF16), t_ni.astype(BF16)], 1))
        c = jnp.dot(jnp.concatenate(ts, 0), w2_ref[...], preferred_element_type=F32)
        re, im = c[:, :SIDE], c[:, SIDE:]
        power = (re * re + im * im) * scale
        p_ref[pl.ds(start, 2 * FR)] = power
        band_ref[...] += power[:FR] + power[FR:]

    @pl.when(step == 0)
    def _():
        barrier = pltpu.get_barrier_semaphore()
        for off in range(1, slabs):
            pl.semaphore_signal(barrier, inc=1, device_id=peer("tm", off), device_id_type=MESH)
        for off in range(1, owner_count):
            pl.semaphore_signal(barrier, inc=1, device_id=peer("dm", off), device_id_type=MESH)
        pl.semaphore_wait(barrier, slabs + owner_count - 2)
        if slabs > 1:
            history_copy().start()
        for tap in range(4):
            filt[tap] = unfold(proto_ref.at[tap : tap + 1], 0)
        band_ref[...] = jnp.zeros_like(band_ref)
        direct[...] = jnp.zeros_like(direct)
        mirror[...] = jnp.zeros_like(mirror)
        for k in range(4):
            early[(k + 3) * SIDE : (k + 4) * SIDE] = unfold(x_ref, k)

    @pl.when(step > 0)
    def _():
        for k in range(4):
            window[(k + 3) * SIDE : (k + 4) * SIDE] = unfold(x_ref, k)
        for s in (0, 2):
            pair(window, s, pl.multiple_of((step * SPB + s) * FR, FR))

    @pl.when(step == 0)
    def _():
        window[4 * SIDE : 7 * SIDE] = early[4 * SIDE : 7 * SIDE]

    for k in range(4, SPB):
        window[(k + 3) * SIDE : (k + 4) * SIDE] = unfold(x_ref, k)
    for s in range(4, SPB, 2):
        pair(window, s, pl.multiple_of((step * SPB + s) * FR, FR))
    window[: 3 * SIDE] = window[SPB * SIDE :]

    @pl.when(step == spec // SPB - 1)
    def _():
        if slabs > 1:
            history_copy().wait()
            for k in range(3):
                early[k * SIDE : (k + 1) * SIDE] = jnp.where(tm > 0, unfold(history, k), 0.0)
        else:
            early[: 3 * SIDE] = jnp.zeros((3 * SIDE, SIDE), F32)
        for s in (0, 2):
            pair(early, s, s * FR)
        finish(
            sizes, peer, m_ref, delays_ref, widths_ref, owners_ref, out_ref,
            p_ref, band_ref, bands, inv, direct, mirror, tot, tail, send, got,
            band_send, band_recv, tail_send, tail_recv, own_send, own_recv,
        )


def finish(
    sizes, peer, m_ref, delays_ref, widths_ref, owners_ref, out_ref,
    p_ref, band_ref, bands, inv, direct, mirror, tot, tail, send, got,
    band_send, band_recv, tail_send, tail_recv, own_send, own_recv,
):
    spectra, spec, groups, slabs, owner_count, axes = sizes
    halo = MAXT * TT + WMAX - 1
    slots = out_ref.shape[0]
    trials = out_ref.shape[2] // widths_ref.shape[1]
    quad = trials * groups
    tm, dm = lax.axis_index("tm"), lax.axis_index("dm")

    copies = []
    for off in range(1, slabs):
        copy = pltpu.make_async_remote_copy(
            src_ref=band_ref,
            dst_ref=bands.at[off - 1],
            send_sem=band_send.at[off - 1],
            recv_sem=band_recv.at[off - 1],
            device_id=peer("tm", off),
            device_id_type=MESH,
        )
        copy.start()
        copies.append(copy)
    iota = lambda shape, dim: lax.broadcasted_iota(jnp.int32, shape, dim)
    spread = (iota((NBLK, SIDE), 1) == 2 * iota((NBLK, SIDE), 0)).astype(BF16)
    late = jnp.dot(delays_ref[...].astype(F32).astype(BF16), spread, preferred_element_type=F32)
    on = iota((quad, SIDE), 1) % 2 == 0
    mask = jnp.concatenate(
        [jnp.where(on & (late == float(v)), 1.0, 0.0) for v in range(MAXT + 1)], 0
    ).astype(BF16)
    def column(ref):
        n = ref.shape[1]
        same = iota((n, n), 0) == iota((n, n), 1)
        return jnp.sum(jnp.where(same, jnp.broadcast_to(ref[...], (n, n)), 0), 1, keepdims=True)

    wide = max(SIDE, quad)
    lane = iota((groups, wide), 1)
    row = iota((groups, wide), 0)
    owner = jnp.broadcast_to(column(owners_ref), (groups, wide))
    mine = jnp.sum(jnp.where(lane // trials == row, owner, 0), 0, keepdims=True)
    rank = jnp.sum(jnp.where((owner == mine) & (row < lane // trials), 1, 0), 0, keepdims=True)
    place = (mine * slots + rank) * trials + lane[:1] % trials
    place = jnp.where(lane[:1] < quad, place, -1)
    rows_out = owner_count * slots * trials
    pack = jnp.where(iota((rows_out, wide), 0) == place, 1.0, 0.0)
    reach = jnp.broadcast_to(column(widths_ref), (widths_ref.shape[1], SIDE))
    root = 1.0 / jnp.sqrt(reach.astype(F32))
    weights = [jnp.where(reach > lag, root, 0.0) for lag in range(WMAX)]

    band = band_ref[...]
    for off in range(1, slabs):
        copies[off - 1].wait()
        band = band + bands[off - 1]
    held = lax.broadcasted_iota(jnp.int32, (FR, SIDE), 0) <= HALF
    inv[...] = jnp.where(held, 1.0 / (band * (1.0 / spectra) + 1e-06), 0.0)

    even = lax.broadcasted_iota(jnp.int32, (FD * groups, SIDE), 1) % 2 == 0

    def block(step, carry):
        for s in range(0, SPB, 2):
            flats = []
            for k in (s, s + 1):
                start = pl.multiple_of((step * SPB + k) * FR, FR)
                ratio = p_ref[pl.ds(start, FR)] * inv[...]
                line = 2.0 * jnp.sum(ratio, 0, keepdims=True) - ratio[:1] - ratio[HALF : HALF + 1]
                mean = jnp.sum(line, 1, keepdims=True) * (1.0 / (SIDE * SIDE))
                flats.append((ratio - mean).astype(BF16))
            r = jnp.dot(m_ref[...], jnp.concatenate(flats, 1), preferred_element_type=F32)
            size = FD * groups
            for m in range(2):
                part = r[:, m * SIDE : (m + 1) * SIDE]
                one = jnp.where(even, part[:size], part[size : 2 * size])
                two = jnp.where(even, part[3 * size :], part[2 * size : 3 * size])
                for d in range(FD):
                    direct[step * SPB + s + m + d] += one[d * groups : (d + 1) * groups]
                    mirror[step * SPB + s + m + d] += two[d * groups : (d + 1) * groups]
        return carry

    def combine(first, stop):
        one = direct[first:stop].reshape(-1, SIDE)
        two = mirror[first:stop].reshape(-1, SIDE)
        high = two.astype(BF16)
        low = (two - high.astype(F32)).astype(BF16)
        both = jnp.concatenate([high, low], 1)
        turned = jnp.dot(both, turn, preferred_element_type=F32)
        total = one + pltpu.roll(one, SIDE - 1, 1) + turned
        tot[first:stop] = total.reshape(stop - first, groups, SIDE)

    source = iota((2 * SIDE, SIDE), 0) % SIDE
    goal = iota((2 * SIDE, SIDE), 1)
    turn = jnp.where((goal % 2 == 0) & (source // 2 == HALF - 1 - goal // 2), 1.0, 0.0).astype(BF16)
    blocks = spec // SPB
    last = -(-(halo + FD - 1) // SPB)
    lax.fori_loop(blocks - last, blocks, block, 0)
    combine(spec - halo, spec + FD - 1)
    if slabs > 1:
        tail_copy = pltpu.make_async_remote_copy(
            src_ref=tot.at[pl.ds(spec - halo, halo + FD - 1)],
            dst_ref=tail,
            send_sem=tail_send,
            recv_sem=tail_recv,
            device_id=peer("tm", 1),
            device_id_type=MESH,
        )
        tail_copy.start()
        lax.fori_loop(0, blocks - last, block, 0)
        combine(0, spec - halo)
        tail_copy.wait()
        before = jnp.where(tm > 0, tail[...], 0.0)
    else:
        lax.fori_loop(0, blocks - last, block, 0)
        combine(0, spec - halo)
        before = jnp.zeros(tail.shape, F32)

    rows = spec + halo + 1
    ext = jnp.concatenate(
        [
            jnp.zeros((1, groups, SIDE), F32),
            before[:halo],
            tot[: FD - 1] + before[halo:],
            tot[FD - 1 : spec],
        ],
        0,
    ).reshape(rows * groups, SIDE)
    width = SIDE * SIDE // NBLK
    sub = (ext * (1.0 / math.sqrt(width))).astype(BF16)
    prod = lax.dot_general(
        sub, mask, (((1,), (1,)), ((), ())), preferred_element_type=F32
    )
    lanes = prod.shape[1]
    prod = prod.reshape(rows, groups, lanes)
    lane = lax.broadcasted_iota(jnp.int32, (groups, lanes), 1)
    row = lax.broadcasted_iota(jnp.int32, (groups, lanes), 0)
    own = (lane // trials) % groups == row
    each = jnp.sum(jnp.where(own[None], prod, 0.0), 1)
    count = spec + TT
    dd = 0.0
    for value in range(MAXT + 1):
        start = (MAXT - value) * TT
        dd = dd + each[start : start + count, value * quad : (value + 1) * quad]
    dd = dd * (1.0 / math.sqrt(NBLK))
    if quad < wide:
        dd = jnp.concatenate([dd, jnp.zeros((count, wide - quad), F32)], 1)
    dd = jnp.concatenate([dd, jnp.zeros((2 * SIDE - count, wide), F32)], 0)
    packed = jnp.dot(
        pack, dd.T, preferred_element_type=F32, precision=lax.Precision.HIGHEST
    )
    send[...] = packed.reshape(send.shape)

    copies = []
    for off in range(1, owner_count):
        copy = pltpu.make_async_remote_copy(
            src_ref=send.at[lax.rem(dm + off, owner_count)],
            dst_ref=got.at[dm],
            send_sem=own_send.at[off - 1],
            recv_sem=own_recv.at[off - 1],
            device_id=peer("dm", off),
            device_id_type=MESH,
        )
        copy.start()
        copies.append(copy)
    got[dm] = send[dm]
    for copy in copies:
        copy.wait()

    for d in range(owner_count):
        part = got[d]
        acc = 0.0
        for lag in range(WMAX):
            moved = pltpu.roll(part, 2 * SIDE - (TT - lag), 1)[:, :SIDE]
            acc = acc + moved[:, None, :] * weights[lag][None]
        for s in range(slots):
            part = acc[s * trials : (s + 1) * trials].reshape(-1, SIDE)
            out_ref[s, d] = part.astype(BF16)


def shards(axes, raw, proto, delays, widths, owners):
    taps, channels = proto.shape
    spec = raw.shape[1] // channels
    groups, trials, _ = delays.shape
    slabs, owner_count = lax.axis_size("tm"), lax.axis_size("dm")
    capacity = 2 * (groups // owner_count)
    halo = MAXT * TT + WMAX - 1
    w1, w2, tw = tables(channels)
    masks = fine_rows(groups, channels // NBLK)
    sizes = (spec * slabs, spec, groups, slabs, owner_count, axes)
    block = pltpu.VMEM((owner_count, capacity * trials, 2 * SIDE), F32)
    sems = lambda n: pltpu.SemaphoreType.DMA((max(n, 1),))
    full = lambda shape: pl.BlockSpec(shape, lambda i: (0,) * len(shape))
    small = [proto, w1, w2, tw, masks, delays.reshape(groups * trials, NBLK), widths[None], owners.T]
    out = (capacity, owner_count, trials * widths.shape[0], spec)
    box = pl.pallas_call(
        functools.partial(search_kernel, sizes),
        grid=(spec // SPB,),
        in_specs=[
            pl.BlockSpec((1, SPB * channels), lambda i: (0, i)),
            pl.BlockSpec(memory_space=pl.ANY),
            *[full(value.shape) for value in small],
        ],
        out_specs=full(out),
        out_shape=jax.ShapeDtypeStruct(out, BF16),
        scratch_shapes=[
            pltpu.VMEM(((SPB + 3) * SIDE, SIDE), F32),
            pltpu.VMEM((7 * SIDE, SIDE), F32),
            pltpu.VMEM((1, 3 * channels), BF16),
            pltpu.VMEM((taps, SIDE, SIDE), F32),
            pltpu.VMEM((spec * FR, SIDE), F32),
            pltpu.VMEM((FR, SIDE), F32),
            pltpu.VMEM((max(slabs - 1, 1), FR, SIDE), F32),
            pltpu.VMEM((FR, SIDE), F32),
            pltpu.VMEM((spec + FD - 1, groups, SIDE), F32),
            pltpu.VMEM((spec + FD - 1, groups, SIDE), F32),
            pltpu.VMEM((spec + FD - 1, groups, SIDE), F32),
            pltpu.VMEM((halo + FD - 1, groups, SIDE), F32),
            block,
            block,
            pltpu.SemaphoreType.DMA,
            pltpu.SemaphoreType.DMA,
            sems(slabs - 1),
            sems(slabs - 1),
            pltpu.SemaphoreType.DMA,
            pltpu.SemaphoreType.DMA,
            sems(owner_count - 1),
            sems(owner_count - 1),
        ],
        compiler_params=pltpu.CompilerParams(
            vmem_limit_bytes=56 << 20, collective_id=0, has_side_effects=True
        ),
        name="search",
    )(raw, raw, *small)
    return box.reshape(capacity, owner_count, 1, trials, widths.shape[0], spec)


def solution(mesh):
    return jax.shard_map(
        functools.partial(shards, mesh.axis_names),
        mesh=mesh,
        in_specs=(P(("group", "dm", "beam"), "tm"), P(), P(), P(), P()),
        out_specs=P("dm", "group", "beam", None, None, "tm"),
        check_vma=False,
    )
```
